512 devices in a mesh: blk: 64 (over z_lo, x, y), grp: 8 (over z_hi, core).
Axes of the slice: x: 4, y: 8, z: 8 (z_hi: 4, z_lo: 2; z = z_hi * 2 + z_lo), core: 2. Of those that a mesh axis runs over, the one named last changes fastest.
Arguments:
- queries: bfloat16 [4096, 32, 128], P(('blk', 'grp')), may hold values from -6 to 6
- query_lens: int32 [4096], P(('blk', 'grp')), may hold values from 8 to 32
- documents: bfloat16 [512, 256, 128], P(('blk', 'grp')), may hold values from -6 to 6
- doc_lens: int32 [512], P(('blk', 'grp')), may hold values from 32 to 256
- positives: int32 [4096], P(('blk', 'grp')), may hold values from 0 to 63
Outputs:
- score_grad: float32 [4096, 3, 128], P(('blk', 'grp'))
- query_losses: float32 [4096, 3], P(('blk', 'grp'))
The draws below stay inside these ranges and needn't reach their ends.
All inputs are finite; a program needn't handle non-finite values.
Results may differ from the reference program's by a relative error of at most 0.00095.
Values may be sent and summed in bfloat16 or wider, within the bound.
A program may use at most 64 MiB of HBM per device.

```python
import jax
import jax.numpy as jnp
from jax import lax

E = 128
QLEN = 32
DLEN = 256
QRY_DEV = 8
DOC_DEV = 1
GROUP_DOCS = 64
CANDIDATES = 128
QUERIES = 4096
DOCUMENTS = 512
N_BLK = 64
N_GRP = 8


def set_ends(drawn, own_key, smallest, top_value):
    dims = drawn.shape
    spot = [jax.random.randint(jax.random.fold_in(own_key, axis), (), 0, dims[axis]) for axis in range(len(dims))]
    drawn = drawn.at[tuple(spot)].set(smallest)
    longest = dims.index(max(dims))
    spot[longest] = (spot[longest] + 1) % dims[longest]
    return drawn.at[tuple(spot)].set(top_value)


def block_levels(rng, shape, split, low, top_value):
    loudness = 1.0
    for dim, blocks in split:
        heights = jax.random.uniform(jax.random.fold_in(jax.random.fold_in(rng, 6), dim), (blocks,), jnp.float32, low / len(split), top_value / len(split))
        loudness = loudness * jnp.repeat(jnp.exp(heights), shape[dim] // blocks).reshape((-1,) + (1,) * (len(shape) - 1 - dim))
    return loudness


def bell_draw(rng, shape, deviation, limit, split=(), kind=jnp.bfloat16):
    values = jax.random.normal(rng, shape, jnp.float32) * deviation
    if len(split) > 0:
        values = block_levels(rng, shape, split, -0.22, 0.18) * values
    return jnp.clip(values, min=-limit, max=limit).astype(kind)


def setup_inputs(seed: int = 0) -> dict:
    splits = jax.random.split(jax.random.key(seed), 6)
    return {
        "queries": bell_draw(splits[0], (QUERIES, QLEN, E), 1.0, 6.0, ((0, 512),)),
        "query_lens": set_ends(jax.random.randint(splits[1], (QUERIES,), QLEN // 4, QLEN + 1), jax.random.fold_in(splits[1], 1), QLEN // 4, QLEN).astype(jnp.int32),
        "documents": bell_draw(splits[2], (DOCUMENTS, DLEN, E), 1.0, 6.0, ((0, 512),)),
        "doc_lens": set_ends(jax.random.randint(splits[3], (DOCUMENTS,), DLEN // 8, DLEN + 1), jax.random.fold_in(splits[3], 1), DLEN // 8, DLEN).astype(jnp.int32),
        "positives": set_ends(jax.random.randint(splits[4], (QUERIES,), 0, GROUP_DOCS), jax.random.fold_in(splits[4], 1), 0, GROUP_DOCS - 1).astype(jnp.int32),
    }


inverse_heat = 0.05
far_below = 1e+30
epsilon = 1e-06
prefixes = (64, 96, 128)

def prefix_norms(tokens):
    values = tokens.astype(jnp.float32)
    squares = values * values
    first = lax.optimization_barrier(jnp.sum(squares[..., :64], axis=-1))
    second = first + lax.optimization_barrier(jnp.sum(squares[..., 64:96], axis=-1))
    third = second + lax.optimization_barrier(jnp.sum(squares[..., 96:], axis=-1))
    return lax.rsqrt(jnp.stack([first, second, third], axis=-1) + epsilon)

def contrast(unnormalized_energies, positives, valid):
    held = jnp.where(valid, unnormalized_energies, -far_below)
    highest = lax.optimization_barrier(jnp.max(held, axis=-1, keepdims=True))
    weights = jnp.where(valid, jnp.exp(held - highest), 0.0)
    totals = lax.optimization_barrier(jnp.sum(weights, axis=-1, keepdims=True))
    columns = lax.broadcasted_iota(jnp.int32, unnormalized_energies.shape, 2)
    target = unnormalized_energies.shape[2] // 2 + positives
    chosen = (columns == target[:, None, None]).astype(unnormalized_energies.dtype)
    picked = lax.optimization_barrier(jnp.sum(unnormalized_energies * chosen, axis=-1))
    losses = jnp.log(totals[..., 0]) + highest[..., 0] - picked
    return (weights / totals - chosen, losses)

def group_scores(query_tok, question_alive_bits, doc_tok, doc_live):
    lane_ordinal, question_span_size, width = query_tok.shape
    rows = query_tok.reshape(lane_ordinal * question_span_size, width)
    row_vector_norms = prefix_norms(rows)

    def one_doc(pair):
        tokens, live = pair
        column_norms = prefix_norms(tokens)
        nested_dimension_weights = []
        for position, prefix in enumerate(prefixes):
            dots = jnp.dot(rows[:, :prefix], tokens[:, :prefix].T, preferred_element_type=jnp.float32)
            cosine = dots * column_norms[:, position][None, :]
            cosine = jnp.where(live[None, :], cosine, -far_below)
            peak_affinity = lax.optimization_barrier(jnp.max(cosine, axis=1)) * row_vector_norms[:, position]
            nested_dimension_weights.append(lax.optimization_barrier(jnp.sum(peak_affinity.reshape(lane_ordinal, question_span_size) * question_alive_bits, axis=1)) / inverse_heat)
        return jnp.stack(nested_dimension_weights, axis=1)
    result = lax.map(one_doc, (doc_tok, doc_live))
    return jnp.transpose(result, (1, 2, 0))

def reference(queries, query_lens, documents, doc_lens, positives):
    query_grid = queries.reshape(N_BLK, N_GRP, QRY_DEV, QLEN, E)
    doc_grid = documents.reshape(N_BLK, N_GRP, DOC_DEV, DLEN, E)
    question_alive_bits = (jnp.arange(QLEN, dtype=jnp.int32)[None, :] < query_lens[:, None]).astype(jnp.float32)
    question_alive_bits = question_alive_bits.reshape(N_BLK, N_GRP, QRY_DEV, QLEN)
    doc_live = (jnp.arange(DLEN, dtype=jnp.int32)[None, :] < doc_lens[:, None]).reshape(N_BLK, N_GRP, DOC_DEV, DLEN)
    target_grid = positives.reshape(N_BLK, N_GRP, QRY_DEV)
    gradients = []
    losses = []
    for cohort_ordinal in range(N_GRP):
        members = query_grid[:, cohort_ordinal].reshape(N_BLK * QRY_DEV, QLEN, E)
        member_live = question_alive_bits[:, cohort_ordinal].reshape(N_BLK * QRY_DEV, QLEN)
        own = group_scores(members, member_live, doc_grid[:, cohort_ordinal].reshape(GROUP_DOCS, DLEN, E), doc_live[:, cohort_ordinal].reshape(GROUP_DOCS, DLEN))
        if cohort_ordinal > 0:
            prior = group_scores(members, member_live, doc_grid[:, cohort_ordinal - 1].reshape(GROUP_DOCS, DLEN, E), doc_live[:, cohort_ordinal - 1].reshape(GROUP_DOCS, DLEN))
        else:
            prior = jnp.zeros_like(own)
        unnormalized_energies = jnp.concatenate([prior, own], axis=2)
        columns = lax.broadcasted_iota(jnp.int32, unnormalized_energies.shape, 2)
        valid = jnp.logical_or(columns >= GROUP_DOCS, cohort_ordinal > 0)
        gradient, loss = contrast(unnormalized_energies, target_grid[:, cohort_ordinal].reshape(N_BLK * QRY_DEV), valid)
        gradients.append(gradient.reshape(N_BLK, QRY_DEV, 3, CANDIDATES))
        losses.append(loss.reshape(N_BLK, QRY_DEV, 3))
    score_grad = jnp.stack(gradients, axis=1).reshape(QUERIES, 3, CANDIDATES)
    query_losses = jnp.stack(losses, axis=1).reshape(QUERIES, 3)
    return (score_grad, query_losses)
```

```python
import functools

import jax
import jax.numpy as jnp
from jax import lax
from jax.experimental import pallas as pl
from jax.experimental.pallas import tpu as pltpu
from jax.sharding import PartitionSpec as P

MESH = pl.DeviceIdType.MESH
F32 = jnp.float32
BF16 = jnp.bfloat16
EPS = 1e-06
FAR = 1e30
HEAT = 20.0
PREFIXES = (64, 96, 128)
NX, NY, NZ = 4, 8, 2
LAST = (((1,), (1,)), ((), ()))


def offset(k):
    return ((k + 1) // 2) * (2 * (k % 2) - 1)


def kernel(
    q_ref, d_ref, qlen_ref, dlen_ref, pos_ref, grad_ref, loss_ref,
    qs, ws, ds, rd, peaks, piece, parts, frame,
    q_send, q_recv, d_send, d_recv, p_send, p_recv, r_send, r_recv,
):
    blk, grp = lax.axis_index("blk"), lax.axis_index("grp")
    zl, x, y = blk // (NX * NY), (blk // NY) % NX, blk % NY
    n_grp = lax.axis_size("grp")

    def at(z_, x_, y_):
        return ((z_ * NX + x_) * NY + y_, grp)

    def along_y(by):
        return at(zl, x, (y + by + NY) % NY)

    def along_xz(a, b):
        return at((zl + a) % NZ, (x + b + NX) % NX, y)

    def remote(src, dst, send, recv, to):
        return pltpu.make_async_remote_copy(
            src_ref=src, dst_ref=dst, send_sem=send, recv_sem=recv, device_id=to, device_id_type=MESH
        )

    plane = [(a, b) for a in range(NZ) for b in range(NX) if (a, b) != (0, 0)]
    after, before = (blk, (grp + 1) % n_grp), (blk, (grp + n_grp - 1) % n_grp)

    barrier = pltpu.get_barrier_semaphore()
    senders = [along_y(by) for by in range(1, NY)] + [along_xz(a, b) for a, b in plane] + [before]
    for other in senders:
        pl.semaphore_signal(barrier, inc=1, device_id=other, device_id_type=MESH)

    tokens = lax.broadcasted_iota(jnp.int32, (32, 128), 0)
    for i in range(8):
        rows = q_ref[pl.ds(32 * i, 32), :].astype(F32)
        qs[0, pl.ds(32 * i, 32), :] = jnp.where(tokens < qlen_ref[i], rows, 0.0).astype(BF16)
    doc = d_ref[...].astype(F32)
    slots = lax.broadcasted_iota(jnp.int32, (256, 128), 0)
    ds[1, 0, 0] = jnp.where(slots < dlen_ref[0], doc, doc[0:1, :]).astype(BF16)

    pl.semaphore_wait(barrier, len(senders))

    def prior_copy():
        return remote(ds.at[1, 0, 0], ds.at[0, 0, 0], p_send.at[0], p_recv.at[0], after)

    def query_copy(k):
        return remote(qs.at[0], qs.at[k], q_send.at[k], q_recv.at[k], along_y(offset(k)))

    def doc_copy(half, a, b):
        i = half * 8 + a * 4 + b
        return remote(ds.at[half, 0, 0], ds.at[half, a, b], d_send.at[i], d_recv.at[i], along_xz(a, b))

    prior_copy().start()
    order = [(0, 1), (0, 3), (1, 0), (0, 2), (1, 1), (1, 3), (1, 2)]
    for k in (1, 2):
        query_copy(k).start()
    for a, b in order:
        doc_copy(1, a, b).start()
    for k in (3, 4, 5, 6, 7):
        query_copy(k).start()

    lanes = lax.broadcasted_iota(jnp.int32, (256, 128), 1)

    def make_weights(k):
        q = qs[k].astype(F32)
        for p in range(2):
            ws[k, p] = jnp.where(lanes < PREFIXES[p], q, 0.0).astype(BF16)
        ws[k, 2] = qs[k]

    make_weights(0)
    prior_copy().wait_recv()
    for a, b in order:
        doc_copy(0, a, b).start()

    def make_norms(half, a, b):
        values = ds[half, a, b].astype(F32)
        squares = values * values
        total = jnp.zeros((256, 1), F32)
        low = 0
        for p, high in enumerate(PREFIXES):
            part = jnp.where((lanes >= low) & (lanes < high), squares, 0.0)
            total = total + jnp.sum(part, axis=1, keepdims=True)
            rd[p, half, a, b] = jnp.broadcast_to(lax.rsqrt(total + EPS), (256, 128))
            low = high

    def job(k, half, a):
        docs = ds[half, a].reshape(1024, 128)
        for p in range(3):
            dots = lax.dot_general(docs, ws[k, p], LAST, preferred_element_type=F32)
            scale = rd[p, half, a].reshape(1024, 128)
            for c in range(2):
                scaled = dots[:, c * 128 : (c + 1) * 128] * scale
                best = jnp.max(scaled.reshape(4, 32, 8, 128), axis=1)
                peaks[k, p, half, a, :, :, pl.ds(c * 128, 128)] = best

    def wait_docs(half, a):
        for b in range(NX):
            if isinstance(a, int) and a == 0 and b == 0:
                continue
            doc_copy(half, a, b).wait_recv()

    prefix_rows = lax.broadcasted_iota(jnp.int32, (8, 128), 0)
    prefix_lanes = lax.broadcasted_iota(jnp.int32, (8, 128), 1)
    limit = jnp.where(prefix_rows == 0, 64, jnp.where(prefix_rows == 1, 96, 128))
    below = (prefix_lanes < limit).astype(F32).astype(BF16)
    seg_rows = lax.broadcasted_iota(jnp.int32, (128, 256), 0)
    seg_query = lax.broadcasted_iota(jnp.int32, (128, 256), 1) // 32

    def split(value):
        high = value.astype(BF16)
        return high, value - high.astype(F32)

    def finish(k):
        q = qs[k].astype(F32)
        high, rest = split(q * q)
        sums = lax.dot_general(below, high, LAST, preferred_element_type=F32)
        sums += lax.dot_general(below, rest.astype(BF16), LAST, preferred_element_type=F32)
        rq = lax.rsqrt(sums + EPS) * HEAT
        total = jnp.zeros((16, 128), F32)
        for p in range(3):
            best = jnp.max(peaks[k, p].reshape(16, 8, 256), axis=1) * rq[p : p + 1, :]
            seg = (seg_rows == seg_query + 8 * p).astype(F32).astype(BF16)
            high, rest = split(best)
            middle, rest = split(rest)
            for part in (high, middle, rest.astype(BF16)):
                total += lax.dot_general(part, seg, LAST, preferred_element_type=F32)
        return total

    def back_copy(k):
        return remote(piece.at[k], parts.at[y], r_send.at[k], r_recv.at[k], along_y(-offset(k)))

    for k in (1, 2):
        query_copy(k).wait_recv()
        make_weights(k)
    for half in (1, 0):
        for a in range(NZ):
            wait_docs(half, a)

            def norms(b, carry):
                make_norms(half, a, b)
                return carry

            lax.fori_loop(0, NX, norms, 0)

            def near(k, carry):
                job(k, half, a)
                return carry

            lax.fori_loop(1, 3, near, 0)

    def send_back(k, carry):
        piece[k] = finish(k)
        back_copy(k).start()
        return carry

    lax.fori_loop(1, 3, send_back, 0)

    def far(k, carry):
        query_copy(k).wait_recv()
        make_weights(k)

        def one(i, inner):
            job(k, i // 2, i % 2)
            return inner

        lax.fori_loop(0, 4, one, 0)
        return send_back(k, carry)

    lax.fori_loop(3, 8, far, 0)

    def own(i, carry):
        job(0, i // 2, i % 2)
        return carry

    lax.fori_loop(0, 4, own, 0)
    parts[y] = finish(0)

    for k in range(1, NY):
        back_copy(k).wait_recv()

    for half in range(2):
        for a in range(NZ):
            for b in range(NX):
                row = half * 8 + a * 4 + b
                column = half * 8 + ((zl + a) % NZ) * 4 + (x - b + NX) % NX
                frame[column] = parts[:, row, :]
    logits = jnp.transpose(frame[...].reshape(128, 128))
    columns = lax.broadcasted_iota(jnp.int32, (8, 128), 1)
    rows = lax.broadcasted_iota(jnp.int32, (8, 128), 0)
    valid = jnp.logical_or(columns >= 64, grp > 0)
    target = jnp.zeros((8, 128), jnp.int32)
    for i in range(8):
        target = jnp.where(rows == i, pos_ref[i] + 64, target)
    chosen = (columns == target).astype(F32)
    for p in range(3):
        value = logits[8 * p : 8 * p + 8, :]
        held = jnp.where(valid, value, -FAR)
        highest = jnp.max(held, axis=1, keepdims=True)
        weights = jnp.where(valid, jnp.exp(held - highest), 0.0)
        total = jnp.sum(weights, axis=1, keepdims=True)
        picked = jnp.sum(jnp.where(columns == target, value, 0.0), axis=1, keepdims=True)
        grad_ref[:, p, :] = weights / total - chosen
        loss_ref[:, p : p + 1] = jnp.log(total) + highest - picked

    prior_copy().wait_send()
    for k in range(1, NY):
        query_copy(k).wait_send()
        back_copy(k).wait_send()
    for half in range(2):
        for a, b in plane:
            doc_copy(half, a, b).wait_send()


def on_device(queries, query_lens, documents, doc_lens, positives):
    vmem = pl.BlockSpec(memory_space=pltpu.VMEM)
    smem = pl.BlockSpec(memory_space=pltpu.SMEM)
    dma = pltpu.SemaphoreType.DMA
    return pl.pallas_call(
        kernel,
        out_shape=(
            jax.ShapeDtypeStruct((8, 3, 128), F32),
            jax.ShapeDtypeStruct((8, 3), F32),
        ),
        in_specs=[vmem, vmem, smem, smem, smem],
        out_specs=(vmem, vmem),
        scratch_shapes=[
            pltpu.VMEM((8, 256, 128), BF16),
            pltpu.VMEM((8, 3, 256, 128), BF16),
            pltpu.VMEM((2, 2, 4, 256, 128), BF16),
            pltpu.VMEM((3, 2, 2, 4, 256, 128), F32),
            pltpu.VMEM((8, 3, 2, 2, 4, 8, 256), F32),
            pltpu.VMEM((8, 16, 128), F32),
            pltpu.VMEM((8, 16, 128), F32),
            pltpu.VMEM((16, 8, 128), F32),
            dma((8,)), dma((8,)), dma((16,)), dma((16,)), dma((1,)), dma((1,)), dma((8,)), dma((8,)),
        ],
        compiler_params=pltpu.CompilerParams(
            collective_id=0, has_side_effects=True, vmem_limit_bytes=48 * 2**20
        ),
        name="late_interaction",
    )(queries.reshape(256, 128), documents.reshape(256, 128), query_lens, doc_lens, positives)


def solution(mesh):
    both = ("blk", "grp")
    return jax.shard_map(
        on_device,
        mesh=mesh,
        in_specs=(P(both, None, None), P(both), P(both, None, None), P(both), P(both)),
        out_specs=(P(both, None, None), P(both, None)),
        check_vma=False,
    )
```

```python
import jax
import jax.numpy as jnp
from jax import lax
from jax.experimental import pallas as pl
from jax.experimental.pallas import tpu as pltpu
from jax.sharding import PartitionSpec as P

MESH = pl.DeviceIdType.MESH
F32 = jnp.float32
BF16 = jnp.bfloat16
EPS = 1e-06
FAR = 1e30
HEAT = 20.0
PREFIXES = (64, 96, 128)
NX, NY, NZ = 4, 8, 2
LAST = (((1,), (1,)), ((), ()))


def offset(k):
    return ((k + 1) // 2) * (2 * (k % 2) - 1)


def unit(s):
    i = (s - 4) // 2
    kind = jnp.where(s < 4, jnp.where(s == 1, 1, 0), jnp.where(s < 14, (i + 1) % 2, s - 14))
    k = jnp.where(s < 4, jnp.maximum(s - 1, 0), jnp.where(s < 14, 1 + 2 * ((i + 1) // 2) + s % 2, 7))
    return kind, k


def kernel(
    q_ref, d_ref, qlen_ref, dlen_ref, pos_ref, grad_ref, loss_ref,
    q_own, d_own, q_mine, d_mine, qs, ws, ds, rd, rq, peaks, piece, parts, frame, in_sem,
    x_sem, z_send, z_recv, ring_send, ring_recv, sib_send, sib_recv, d_send, d_recv, r_send, r_recv,
):
    blk, grp = lax.axis_index("blk"), lax.axis_index("grp")
    zl, x, y = blk // (NX * NY), (blk // NY) % NX, blk % NY
    slab, core = grp // 2, grp % 2
    slabs = lax.axis_size("grp") // 2
    direct = zl == core
    kind = jnp.where(direct, 0, 1)
    half = 1 - kind
    older = jnp.logical_and(zl == 0, core == 1)
    fetch = jnp.logical_and(older, slab > 0)
    keeps = jnp.logical_not(fetch)
    hands_on = jnp.logical_and(core == 1, slab < slabs - 1)
    to_partner = jnp.logical_not(jnp.logical_and(zl == 1, core == 1))
    from_partner = jnp.logical_not(older)
    first = jnp.maximum(zl, core)

    def at(z_, x_, y_, slab_, core_):
        return ((z_ * NX + x_) * NY + y_, slab_ * 2 + core_)

    def along_y(by):
        return at(zl, x, (y + by + NY) % NY, slab, core)

    def along_x(by):
        return at(zl, (x + by + NX) % NX, y, slab, core)

    sibling = at(zl, x, y, slab, 1 - core)
    partner = at(1 - zl, x, y, slab, core)
    crossed = at(1 - zl, x, y, slab, 1 - core)
    ahead = at(0, x, y, slab + 1, 1)

    def remote(src, dst, send, recv, to):
        return pltpu.make_async_remote_copy(
            src_ref=src, dst_ref=dst, send_sem=send, recv_sem=recv, device_id=to, device_id_type=MESH
        )

    loads = [
        pltpu.make_async_copy(q_ref, q_own, in_sem.at[0]),
        pltpu.make_async_copy(d_ref, d_own, in_sem.at[1]),
    ]
    for load in loads:
        load.start()

    barrier = pltpu.get_barrier_semaphore()

    def greet(other):
        pl.semaphore_signal(barrier, inc=1, device_id=other, device_id_type=MESH)

    for other in (along_y(1), along_y(-1), sibling, along_x(1), along_x(-1), along_x(2)):
        greet(other)
    pl.when(from_partner)(lambda: greet(partner))
    pl.when(kind == 1)(lambda: greet(crossed))

    @pl.when(fetch)
    def _():
        greet(at(0, x, y, slab - 1, 1))
        greet(at(1, x, y, slab - 1, 1))

    expected = 6 + to_partner.astype(jnp.int32) + kind + hands_on.astype(jnp.int32)

    for load in loads:
        load.wait()

    tokens = lax.broadcasted_iota(jnp.int32, (32, 128), 0)
    for i in range(8):
        rows = q_own[pl.ds(32 * i, 32), :].astype(F32)
        q_mine[pl.ds(32 * i, 32), :] = jnp.where(tokens < qlen_ref[i], rows, 0.0).astype(BF16)
    doc = d_own[...].astype(F32)
    slots = lax.broadcasted_iota(jnp.int32, (256, 128), 0)
    d_mine[...] = jnp.where(slots < dlen_ref[0], doc, doc[0:1, :]).astype(BF16)

    @pl.when(direct)
    def _():
        qs[0, 0] = q_mine[...]

    @pl.when(keeps)
    def _():
        ds[zl, 0] = d_mine[...]

    @pl.when(jnp.logical_and(keeps, older))
    def _():
        ds[1, 0] = d_mine[...]

    pl.semaphore_wait(barrier, expected)

    def cross_copy():
        return remote(q_mine, qs.at[1, 0], x_sem.at[0], x_sem.at[1], crossed)

    def partner_copy():
        return remote(d_mine, ds.at[zl, 0], z_send.at[0], z_recv.at[0], partner)

    def ahead_copy():
        return remote(d_mine, ds.at[zl, 0], z_send.at[1], z_recv.at[1 + zl], ahead)

    def behind_copy(slot):
        return remote(d_mine, ds.at[slot, 0], z_send.at[1], z_recv.at[1 + slot], ahead)

    def ring_copy(k):
        if k == 7:
            rows = pl.ds(0, 128)
            return remote(
                qs.at[kind, 5, rows], qs.at[kind, 7, rows], ring_send.at[7], ring_recv.at[7], along_y(1)
            )
        if k == 8:
            rows = pl.ds(128, 128)
            return remote(
                qs.at[kind, 6, rows], qs.at[kind, 7, rows], ring_send.at[8], ring_recv.at[8], along_y(-1)
            )
        return remote(
            qs.at[kind, max(k - 2, 0)], qs.at[kind, k], ring_send.at[k], ring_recv.at[k],
            along_y(1 if k % 2 else -1),
        )

    def sib_copy(k):
        return remote(qs.at[kind, k], qs.at[kind, k], sib_send.at[k], sib_recv.at[k], sibling)

    def sib_wait(k):
        remote(qs.at[1 - kind, k], qs.at[1 - kind, k], sib_send.at[k], sib_recv.at[k], sibling).wait_recv()

    def doc_copy(slot, b):
        return remote(ds.at[slot, 0], ds.at[slot, b], d_send.at[slot, b], d_recv.at[slot, b], along_x(b))

    def enter():
        ring_copy(1).start()
        ring_copy(2).start()
        sib_copy(0).start()

    def pass_on(arrived, onward):
        for k in arrived:
            ring_copy(k).wait_recv()
        for k in onward:
            ring_copy(k).start()
        for k in arrived:
            if k < 8:
                sib_copy(k).start()

    def spread(slot):
        for b in (1, 3, 2):
            doc_copy(slot, b).start()

    pl.when(kind == 1)(lambda: cross_copy().start())
    pl.when(direct)(enter)
    pl.when(to_partner)(lambda: partner_copy().start())
    pl.when(hands_on)(lambda: ahead_copy().start())

    @pl.when(keeps)
    def _():
        spread(first)

    @pl.when(jnp.logical_and(keeps, older))
    def _():
        spread(1 - first)

    @pl.when(kind == 1)
    def _():
        cross_copy().wait_recv()
        enter()

    @pl.when(fetch)
    def _():
        behind_copy(1).wait_recv()
        spread(1)
        behind_copy(0).wait_recv()
        spread(0)

    @pl.when(from_partner)
    def _():
        remote(d_mine, ds.at[1 - zl, 0], z_send.at[0], z_recv.at[0], partner).wait_recv()
        spread(1 - zl)

    lanes = lax.broadcasted_iota(jnp.int32, (256, 128), 1)
    prefix_rows = lax.broadcasted_iota(jnp.int32, (8, 128), 0)
    prefix_lanes = lax.broadcasted_iota(jnp.int32, (8, 128), 1)
    limit = jnp.where(prefix_rows == 0, 64, jnp.where(prefix_rows == 1, 96, 128))
    below = (prefix_lanes < limit).astype(F32).astype(BF16)
    seg_rows = lax.broadcasted_iota(jnp.int32, (128, 256), 0)
    seg_query = lax.broadcasted_iota(jnp.int32, (128, 256), 1) // 32

    def split(value):
        high = value.astype(BF16)
        return high, value - high.astype(F32)

    def prepare(s):
        kind_, k = unit(s)
        q = qs[kind_, k].astype(F32)
        for p in range(2):
            ws[s, p] = jnp.where(lanes < PREFIXES[p], q, 0.0).astype(BF16)
        ws[s, 2] = qs[kind_, k]
        high, rest = split(q * q)
        sums = lax.dot_general(below, high, LAST, preferred_element_type=F32)
        sums += lax.dot_general(below, rest.astype(BF16), LAST, preferred_element_type=F32)
        rq[s] = lax.rsqrt(sums + EPS) * HEAT

    wide_rows = lax.broadcasted_iota(jnp.int32, (256, 128), 0)
    ones = (lanes < jnp.where(wide_rows < 128, 64, 96)).astype(F32).astype(BF16)

    def norms(slot):
        values = ds[slot].reshape(1024, 128).astype(F32)
        squares = values * values
        high, rest = split(squares)
        sums = lax.dot_general(high, ones, LAST, preferred_element_type=F32)
        sums += lax.dot_general(rest.astype(BF16), ones, LAST, preferred_element_type=F32)
        for p in range(2):
            rd[p, slot] = lax.rsqrt(sums[:, 128 * p : 128 * p + 128] + EPS)
        total = jnp.sum(squares, axis=1, keepdims=True)
        rd[2, slot] = jnp.broadcast_to(lax.rsqrt(total + EPS), (1024, 128))

    def job(s, slot):
        docs = ds[slot].reshape(1024, 128)
        for p in range(3):
            dots = lax.dot_general(docs, ws[s, p], LAST, preferred_element_type=F32)
            scale = rd[p, slot]
            for c in range(2):
                scaled = dots[:, c * 128 : (c + 1) * 128] * scale
                best = jnp.max(jnp.max(scaled.reshape(4, 32, 8, 128), axis=1), axis=1)
                peaks[s, p, slot, :, pl.ds(c * 128, 128)] = best

    def finish(s):
        total = jnp.zeros((8, 128), F32)
        for p in range(3):
            best = peaks[s, p].reshape(8, 256) * rq[s, p : p + 1, :]
            seg = (seg_rows == seg_query + 8 * p).astype(F32).astype(BF16)
            high, rest = split(best)
            middle, rest = split(rest)
            for part in (high, middle, rest.astype(BF16)):
                total += lax.dot_general(part, seg, LAST, preferred_element_type=F32)
        piece[s] = total

    def back_copy(s):
        kind_, k = unit(s)
        home = at(jnp.where(kind_ == 0, zl, 1 - zl), x, (y - offset(k) + NY) % NY, slab, zl)
        return remote(piece.at[s], parts.at[half, y], r_send.at[s], r_recv.at[half, k], home)

    def is_home(s):
        return jnp.logical_and(direct, s == 0)

    def send_back(s):
        pl.when(jnp.logical_not(is_home(s)))(lambda: back_copy(s).start())

        @pl.when(is_home(s))
        def _():
            parts[half, y] = piece[s]

    @pl.when(direct)
    def _():
        pass_on((1, 2), (3, 4))
        sib_wait(0)

    @pl.when(kind == 1)
    def _():
        for k in range(3):
            sib_wait(k)

    for s in range(4):
        prepare(jnp.int32(s))

    def early(j, carry):
        slot = jnp.where(j == 0, first, 1 - first)
        for b in range(1, NX):
            doc_copy(slot, b).wait_recv()
        norms(slot)
        for s in range(4):
            job(s, slot)

        @pl.when(j == 0)
        def _():
            pl.when(kind == 1)(lambda: pass_on((1, 2), (3, 4)))
            pl.when(direct)(lambda: pass_on((3, 4), (5, 6)))

        return carry

    lax.fori_loop(0, 2, early, 0)

    def later(i, carry):
        s = 4 + 2 * i
        kind_, k = unit(s)

        @pl.when(i == 1)
        def _():
            pl.when(direct)(lambda: pass_on((5, 6), (7, 8)))
            pl.when(kind == 1)(lambda: pass_on((3, 4), (5, 6)))

        @pl.when(i == 3)
        def _():
            pl.when(direct)(lambda: pass_on((8, 7), ()))
            pl.when(kind == 1)(lambda: pass_on((5, 6), (7, 8)))

        @pl.when(kind_ != kind)
        def _():
            sib_wait(k)
            sib_wait(k + 1)

        finish(2 * i)
        finish(2 * i + 1)
        for j in range(2):
            prepare(s + j)
            for slot in range(2):
                job(s + j, slot)
        send_back(2 * i)
        send_back(2 * i + 1)
        return carry

    lax.fori_loop(0, 5, later, 0)

    pl.when(kind == 1)(lambda: pass_on((8, 7), ()))

    def last(i, carry):
        s = 14 + i
        kind_, k = unit(s)
        pl.when(kind_ != kind)(lambda: sib_wait(k))
        finish(10 + 2 * i)
        finish(11 + 2 * i)
        prepare(s)
        for slot in range(2):
            job(s, slot)
        send_back(10 + 2 * i)
        send_back(11 + 2 * i)
        return carry

    lax.fori_loop(0, 2, last, 0)
    finish(14)
    finish(15)
    send_back(jnp.int32(14))
    send_back(jnp.int32(15))

    for h in range(2):
        for k in range(NY):
            back = remote(piece.at[0], parts.at[h, (y + offset(k) + NY) % NY], r_send.at[0], r_recv.at[h, k], sibling)
            if h == 1 and k == 0:
                pl.when(kind == 1)(lambda: back.wait_recv())
            else:
                back.wait_recv()

    for h in range(2):
        for slot in range(NZ):
            for b in range(NX):
                column = h * 8 + slot * 4 + (x - b + NX) % NX
                frame[column] = parts[h, :, slot * 4 + b, :]
    logits = jnp.transpose(frame[...].reshape(128, 128))
    columns = lax.broadcasted_iota(jnp.int32, (8, 128), 1)
    rows = lax.broadcasted_iota(jnp.int32, (8, 128), 0)
    valid = jnp.logical_or(columns >= 64, grp > 0)
    target = jnp.zeros((8, 128), jnp.int32)
    for i in range(8):
        target = jnp.where(rows == i, pos_ref[i] + 64, target)
    chosen = (columns == target).astype(F32)
    for p in range(3):
        value = logits[8 * p : 8 * p + 8, :]
        held = jnp.where(valid, value, -FAR)
        highest = jnp.max(held, axis=1, keepdims=True)
        weights = jnp.where(valid, jnp.exp(held - highest), 0.0)
        total = jnp.sum(weights, axis=1, keepdims=True)
        picked = jnp.sum(jnp.where(columns == target, value, 0.0), axis=1, keepdims=True)
        grad_ref[p] = weights / total - chosen
        losses = jnp.where(columns == rows, jnp.log(total) + highest - picked, 0.0)
        loss_ref[p : p + 1, :] = jnp.sum(losses, axis=0, keepdims=True)[:, :8]

    pl.when(kind == 1)(lambda: cross_copy().wait_send())
    pl.when(to_partner)(lambda: partner_copy().wait_send())
    pl.when(hands_on)(lambda: ahead_copy().wait_send())
    for k in range(1, 9):
        ring_copy(k).wait_send()
    for k in range(NY):
        sib_copy(k).wait_send()
    for slot in range(2):
        for b in range(1, NX):
            doc_copy(slot, b).wait_send()

    def sent(s, carry):
        pl.when(jnp.logical_not(is_home(s)))(lambda: back_copy(s).wait_send())
        return carry

    lax.fori_loop(0, 16, sent, 0)


def on_device(queries, query_lens, documents, doc_lens, positives):
    vmem = pl.BlockSpec(memory_space=pltpu.VMEM)
    hbm = pl.BlockSpec(memory_space=pl.ANY)
    smem = pl.BlockSpec(memory_space=pltpu.SMEM)
    dma = pltpu.SemaphoreType.DMA
    grad, loss = pl.pallas_call(
        kernel,
        out_shape=(
            jax.ShapeDtypeStruct((3, 8, 128), F32),
            jax.ShapeDtypeStruct((3, 8), F32),
        ),
        in_specs=[hbm, hbm, smem, smem, smem],
        out_specs=(vmem, vmem),
        scratch_shapes=[
            pltpu.VMEM((256, 128), BF16),
            pltpu.VMEM((256, 128), BF16),
            pltpu.VMEM((256, 128), BF16),
            pltpu.VMEM((256, 128), BF16),
            pltpu.VMEM((2, 8, 256, 128), BF16),
            pltpu.VMEM((16, 3, 256, 128), BF16),
            pltpu.VMEM((2, 4, 256, 128), BF16),
            pltpu.VMEM((3, 2, 1024, 128), F32),
            pltpu.VMEM((16, 8, 256), F32),
            pltpu.VMEM((16, 3, 2, 4, 256), F32),
            pltpu.VMEM((16, 8, 128), F32),
            pltpu.VMEM((2, 8, 8, 128), F32),
            pltpu.VMEM((16, 8, 128), F32),
            dma((2,)), dma((2,)), dma((2,)), dma((3,)), dma((9,)), dma((9,)), dma((8,)), dma((8,)),
            dma((2, 4)), dma((2, 4)), dma((16,)), dma((2, 8)),
        ],
        compiler_params=pltpu.CompilerParams(
            collective_id=0, has_side_effects=True, vmem_limit_bytes=60 * 2**20
        ),
        name="late_interaction",
    )(queries.reshape(256, 128), documents.reshape(256, 128), query_lens, doc_lens, positives)
    return jnp.transpose(grad, (1, 0, 2)), jnp.transpose(loss)


def solution(mesh):
    both = ("blk", "grp")
    return jax.shard_map(
        on_device,
        mesh=mesh,
        in_specs=(P(both, None, None), P(both), P(both, None, None), P(both), P(both)),
        out_specs=(P(both, None, None), P(both, None)),
        check_vma=False,
    )
```

```python
import jax
import jax.numpy as jnp
from jax import lax
from jax.experimental import pallas as pl
from jax.experimental.pallas import tpu as pltpu
from jax.sharding import PartitionSpec as P

MESH = pl.DeviceIdType.MESH
F32 = jnp.float32
BF16 = jnp.bfloat16
EPS = 1e-06
FAR = 1e30
HEAT = 20.0
PREFIXES = (64, 96, 128)
NX, NY, NZ = 4, 8, 2
LAST = (((1,), (1,)), ((), ()))


def offset(k):
    return ((k + 1) // 2) * (2 * (k % 2) - 1)


def unit(s):
    kind = jnp.where(s < 6, jnp.where((s == 1) | (s > 3), 1, 0), jnp.where(s < 14, ((s - 6) // 2) % 2, s - 14))
    near = jnp.where(s < 2, 0, 1 + s % 2)
    k = jnp.where(s < 6, near, jnp.where(s < 14, 3 + 2 * ((s - 6) // 4) + s % 2, 7))
    return kind, k


def kernel(
    q_ref, d_ref, qlen_ref, dlen_ref, pos_ref, grad_ref, loss_ref,
    q_own, d_own, q_mine, d_mine, qs, ws, ds, rd, rq, peaks, piece, parts, frame, in_sem,
    z_send, z_recv, q_send, q_recv, sib_send, sib_recv, d_send, d_recv, r_send, r_recv,
):
    blk, grp = lax.axis_index("blk"), lax.axis_index("grp")
    zl, x, y = blk // (NX * NY), (blk // NY) % NX, blk % NY
    slab, core = grp // 2, grp % 2
    slabs = lax.axis_size("grp") // 2
    direct = zl == core
    kind = jnp.where(direct, 0, 1)
    half = 1 - kind
    older = jnp.logical_and(zl == 0, core == 1)
    fetch = jnp.logical_and(older, slab > 0)
    keeps = jnp.logical_not(fetch)
    hands_on = jnp.logical_and(core == 1, slab < slabs - 1)
    to_partner = jnp.logical_not(jnp.logical_and(zl == 1, core == 1))
    from_partner = jnp.logical_not(older)
    first = jnp.maximum(zl, core)

    def at(z_, x_, y_, slab_, core_):
        return ((z_ * NX + x_) * NY + y_, slab_ * 2 + core_)

    def along_y(by):
        return at(zl, x, (y + by + NY) % NY, slab, core)

    def along_x(by):
        return at(zl, (x + by + NX) % NX, y, slab, core)

    sibling = at(zl, x, y, slab, 1 - core)
    partner = at(1 - zl, x, y, slab, core)

    def crossed(by):
        return at(1 - zl, x, (y + by + NY) % NY, slab, 1 - core)

    ahead = at(0, x, y, slab + 1, 1)

    def remote(src, dst, send, recv, to):
        return pltpu.make_async_remote_copy(
            src_ref=src, dst_ref=dst, send_sem=send, recv_sem=recv, device_id=to, device_id_type=MESH
        )

    loads = [
        pltpu.make_async_copy(q_ref, q_own, in_sem.at[0]),
        pltpu.make_async_copy(d_ref, d_own, in_sem.at[1]),
    ]
    for load in loads:
        load.start()

    barrier = pltpu.get_barrier_semaphore()

    def greet(other):
        pl.semaphore_signal(barrier, inc=1, device_id=other, device_id_type=MESH)

    for other in (sibling, along_x(1), along_x(-1), along_x(2)):
        greet(other)
    pl.when(from_partner)(lambda: greet(partner))

    for by in (1, -1, 2, -2):
        greet(along_y(by))

    @pl.when(kind == 1)
    def _():
        for by in (0, 1, -1, 2, -2):
            greet(crossed(by))

    @pl.when(fetch)
    def _():
        greet(at(0, x, y, slab - 1, 1))
        greet(at(1, x, y, slab - 1, 1))

    expected = 8 + to_partner.astype(jnp.int32) + 5 * kind + hands_on.astype(jnp.int32)

    for load in loads:
        load.wait()

    tokens = lax.broadcasted_iota(jnp.int32, (32, 128), 0)
    for i in range(8):
        rows = q_own[pl.ds(32 * i, 32), :].astype(F32)
        q_mine[pl.ds(32 * i, 32), :] = jnp.where(tokens < qlen_ref[i], rows, 0.0).astype(BF16)
    doc = d_own[...].astype(F32)
    slots = lax.broadcasted_iota(jnp.int32, (256, 128), 0)
    d_mine[...] = jnp.where(slots < dlen_ref[0], doc, doc[0:1, :]).astype(BF16)

    @pl.when(direct)
    def _():
        qs[0, 0] = q_mine[...]

    @pl.when(keeps)
    def _():
        ds[zl, 0] = d_mine[...]

    @pl.when(jnp.logical_and(keeps, older))
    def _():
        ds[1, 0] = d_mine[...]

    pl.semaphore_wait(barrier, expected)

    def partner_copy():
        return remote(d_mine, ds.at[zl, 0], z_send.at[0], z_recv.at[0], partner)

    def ahead_copy():
        return remote(d_mine, ds.at[zl, 0], z_send.at[1], z_recv.at[1 + zl], ahead)

    def behind_copy(slot):
        return remote(d_mine, ds.at[slot, 0], z_send.at[1], z_recv.at[1 + slot], ahead)

    def query_copy(k):
        return remote(q_mine, qs.at[0, k], q_send.at[k], q_recv.at[k], along_y(offset(k)))

    def cross_copy(k):
        return remote(q_mine, qs.at[1, k], q_send.at[k], q_recv.at[k], crossed(offset(k)))

    def ring_copy(k):
        low, high = pl.ds(0, 128), pl.ds(128, 128)
        if k == 7:
            src, dst, by = qs.at[kind, 3, low], qs.at[kind, 7, low], 2
        elif k == 8:
            src, dst, by = qs.at[kind, 4, high], qs.at[kind, 7, high], -2
        else:
            src, dst, by = qs.at[kind, k - 2], qs.at[kind, k], 1 if k == 5 else -1
        return remote(src, dst, q_send.at[k], q_recv.at[k], along_y(by))

    def sib_copy(k):
        return remote(qs.at[kind, k], qs.at[kind, k], sib_send.at[k], sib_recv.at[k], sibling)

    def sib_wait(k):
        remote(qs.at[1 - kind, k], qs.at[1 - kind, k], sib_send.at[k], sib_recv.at[k], sibling).wait_recv()

    def doc_copy(slot, b):
        return remote(ds.at[slot, 0], ds.at[slot, b], d_send.at[slot, b], d_recv.at[slot, b], along_x(b))

    def arrived(*ks):
        for k in ks:
            (ring_copy if k > 4 else query_copy)(k).wait_recv()
        if 3 in ks:
            for k in (5, 6, 7, 8):
                ring_copy(k).start()
        for k in ks:
            if k < 8:
                sib_copy(k).start()

    def shared(*ks):
        for k in ks:
            sib_wait(k)

    def spread(slot):
        for b in (1, 3, 2):
            doc_copy(slot, b).start()

    pl.when(to_partner)(lambda: partner_copy().start())
    pl.when(hands_on)(lambda: ahead_copy().start())

    @pl.when(direct)
    def _():
        for k in (1, 2):
            query_copy(k).start()

    @pl.when(kind == 1)
    def _():
        for k in range(3):
            cross_copy(k).start()

    @pl.when(keeps)
    def _():
        spread(first)

    @pl.when(jnp.logical_and(keeps, older))
    def _():
        spread(1 - first)

    @pl.when(direct)
    def _():
        sib_copy(0).start()
        for k in (3, 4):
            query_copy(k).start()

    @pl.when(kind == 1)
    def _():
        for k in (3, 4):
            cross_copy(k).start()

    @pl.when(fetch)
    def _():
        behind_copy(1).wait_recv()
        spread(1)
        behind_copy(0).wait_recv()
        spread(0)

    @pl.when(from_partner)
    def _():
        remote(d_mine, ds.at[1 - zl, 0], z_send.at[0], z_recv.at[0], partner).wait_recv()
        spread(1 - zl)

    lanes = lax.broadcasted_iota(jnp.int32, (256, 128), 1)
    prefix_rows = lax.broadcasted_iota(jnp.int32, (8, 128), 0)
    prefix_lanes = lax.broadcasted_iota(jnp.int32, (8, 128), 1)
    limit = jnp.where(prefix_rows == 0, 64, jnp.where(prefix_rows == 1, 96, 128))
    below = (prefix_lanes < limit).astype(F32).astype(BF16)
    seg_rows = lax.broadcasted_iota(jnp.int32, (128, 256), 0)
    seg_query = lax.broadcasted_iota(jnp.int32, (128, 256), 1) // 32

    def split(value):
        high = value.astype(BF16)
        return high, value - high.astype(F32)

    def prepare(s):
        kind_, k = unit(s)
        q = qs[kind_, k].astype(F32)
        for p in range(2):
            ws[s, p] = jnp.where(lanes < PREFIXES[p], q, 0.0).astype(BF16)
        ws[s, 2] = qs[kind_, k]
        high, rest = split(q * q)
        sums = lax.dot_general(below, high, LAST, preferred_element_type=F32)
        sums += lax.dot_general(below, rest.astype(BF16), LAST, preferred_element_type=F32)
        rq[s] = lax.rsqrt(sums + EPS) * HEAT

    wide_rows = lax.broadcasted_iota(jnp.int32, (256, 128), 0)
    ones = (lanes < jnp.where(wide_rows < 128, 64, 96)).astype(F32).astype(BF16)

    def norms(slot):
        values = ds[slot].reshape(1024, 128).astype(F32)
        squares = values * values
        high, rest = split(squares)
        sums = lax.dot_general(high, ones, LAST, preferred_element_type=F32)
        sums += lax.dot_general(rest.astype(BF16), ones, LAST, preferred_element_type=F32)
        for p in range(2):
            rd[p, slot] = lax.rsqrt(sums[:, 128 * p : 128 * p + 128] + EPS)
        total = jnp.sum(squares, axis=1, keepdims=True)
        rd[2, slot] = jnp.broadcast_to(lax.rsqrt(total + EPS), (1024, 128))

    def job(s, slot):
        docs = ds[slot].reshape(1024, 128)
        for p in range(3):
            dots = lax.dot_general(docs, ws[s, p], LAST, preferred_element_type=F32)
            scale = rd[p, slot]
            for c in range(2):
                scaled = dots[:, c * 128 : (c + 1) * 128] * scale
                best = jnp.max(jnp.max(scaled.reshape(4, 32, 8, 128), axis=1), axis=1)
                peaks[s, p, slot, :, pl.ds(c * 128, 128)] = best

    def whole_job(s):
        docs = ds[...].reshape(2048, 128)
        for p in range(3):
            dots = lax.dot_general(docs, ws[s, p], LAST, preferred_element_type=F32)
            scale = rd[p].reshape(2048, 128)
            for c in range(2):
                scaled = dots[:, c * 128 : (c + 1) * 128] * scale
                best = jnp.max(jnp.max(scaled.reshape(2, 4, 32, 8, 128), axis=2), axis=2)
                peaks[s, p, :, :, pl.ds(c * 128, 128)] = best

    def finish(s):
        total = jnp.zeros((16, 128), F32)
        for p in range(3):
            best = jnp.concatenate(
                [peaks[s + j, p].reshape(8, 256) * rq[s + j, p : p + 1, :] for j in range(2)], axis=0
            )
            seg = (seg_rows == seg_query + 8 * p).astype(F32).astype(BF16)
            high, rest = split(best)
            middle, rest = split(rest)
            parts_ = jnp.concatenate([high, middle, rest.astype(BF16)], axis=0)
            sums = lax.dot_general(parts_, seg, LAST, preferred_element_type=F32)
            total += sums[:16] + sums[16:32] + sums[32:]
        piece[s] = total[:8]
        piece[s + 1] = total[8:]

    def back_copy(s):
        kind_, k = unit(s)
        home = at(jnp.where(kind_ == 0, zl, 1 - zl), x, (y - offset(k) + NY) % NY, slab, zl)
        return remote(piece.at[s], parts.at[half, y], r_send.at[s], r_recv.at[half, k], home)

    def is_home(s):
        return jnp.logical_and(direct, s == 0)

    def send_back(s):
        pl.when(jnp.logical_not(is_home(s)))(lambda: back_copy(s).start())

        @pl.when(is_home(s))
        def _():
            parts[half, y] = piece[s]

    @pl.when(direct)
    def _():
        arrived(1, 2)
        shared(0)

    @pl.when(kind == 1)
    def _():
        arrived(0)
        shared(0, 1, 2)
        arrived(1, 2)

    def wait_docs(slot):
        for b in range(1, NX):
            doc_copy(slot, b).wait_recv()

    for s in range(4):
        prepare(jnp.int32(s))
    wait_docs(first)
    norms(first)
    for s in range(4):
        job(s, first)
    pl.when(direct)(lambda: shared(1, 2))
    for s in range(4, 6):
        prepare(jnp.int32(s))
        job(s, first)
    wait_docs(1 - first)
    pl.when(direct)(lambda: arrived(3, 4))
    norms(1 - first)
    for s in range(2, 4):
        job(s, 1 - first)

    def later(i, carry):
        s = 6 + 2 * i
        done = jnp.where(i == 0, 2, 4 + 2 * i)

        @pl.when(kind == 1)
        def _():
            @pl.when(i == 0)
            def _():
                shared(3, 4)
                arrived(3, 4)

            @pl.when(i == 2)
            def _():
                shared(5, 6)
                arrived(5, 6)

            pl.when(i == 3)(lambda: arrived(8, 7))
            pl.when(i == 4)(lambda: shared(7))

        @pl.when(direct)
        def _():
            @pl.when(i == 1)
            def _():
                shared(3, 4)
                arrived(5, 6)

            @pl.when(i == 3)
            def _():
                shared(5, 6)
                arrived(8, 7)

            pl.when(i == 4)(lambda: shared(7))

        finish(done)
        for j in range(2):
            prepare(s + j)
            whole_job(s + j)
        send_back(done)
        send_back(done + 1)
        return carry

    lax.fori_loop(0, 5, later, 0)

    finish(14)
    send_back(jnp.int32(14))
    send_back(jnp.int32(15))
    for s in (4, 5):
        job(s, 1 - first)
    finish(4)
    for s in (4, 5):
        send_back(jnp.int32(s))
    for s in (0, 1):
        job(s, 1 - first)
    finish(0)
    for s in (0, 1):
        send_back(jnp.int32(s))

    for h in range(2):
        for k in range(NY):
            back = remote(piece.at[0], parts.at[h, (y + offset(k) + NY) % NY], r_send.at[0], r_recv.at[h, k], sibling)
            if h == 1 and k == 0:
                pl.when(kind == 1)(lambda: back.wait_recv())
            else:
                back.wait_recv()

    for h in range(2):
        for slot in range(NZ):
            for b in range(NX):
                column = h * 8 + slot * 4 + (x - b + NX) % NX
                frame[column] = parts[h, :, slot * 4 + b, :]
    logits = jnp.transpose(frame[...].reshape(128, 128))
    columns = lax.broadcasted_iota(jnp.int32, (8, 128), 1)
    rows = lax.broadcasted_iota(jnp.int32, (8, 128), 0)
    valid = jnp.logical_or(columns >= 64, grp > 0)
    target = jnp.zeros((8, 128), jnp.int32)
    for i in range(8):
        target = jnp.where(rows == i, pos_ref[i] + 64, target)
    chosen = (columns == target).astype(F32)
    for p in range(3):
        value = logits[8 * p : 8 * p + 8, :]
        held = jnp.where(valid, value, -FAR)
        highest = jnp.max(held, axis=1, keepdims=True)
        weights = jnp.where(valid, jnp.exp(held - highest), 0.0)
        total = jnp.sum(weights, axis=1, keepdims=True)
        picked = jnp.sum(jnp.where(columns == target, value, 0.0), axis=1, keepdims=True)
        grad_ref[:, p, :] = weights / total - chosen
        loss_ref[:, p : p + 1] = jnp.log(total) + highest - picked

    pl.when(kind == 1)(lambda: cross_copy(0).wait_send())
    pl.when(to_partner)(lambda: partner_copy().wait_send())
    pl.when(hands_on)(lambda: ahead_copy().wait_send())
    for k in range(1, 5):
        query_copy(k).wait_send()
    for k in range(5, 9):
        ring_copy(k).wait_send()
    for k in range(NY):
        sib_copy(k).wait_send()
    for slot in range(2):
        for b in range(1, NX):
            doc_copy(slot, b).wait_send()

    def sent(s, carry):
        pl.when(jnp.logical_not(is_home(s)))(lambda: back_copy(s).wait_send())
        return carry

    lax.fori_loop(0, 16, sent, 0)


def on_device(queries, query_lens, documents, doc_lens, positives):
    vmem = pl.BlockSpec(memory_space=pltpu.VMEM)
    hbm = pl.BlockSpec(memory_space=pltpu.HBM)
    smem = pl.BlockSpec(memory_space=pltpu.SMEM)
    dma = pltpu.SemaphoreType.DMA
    far = [
        pltpu.with_memory_space_constraint(block.reshape(256, 128), pltpu.HBM)
        for block in (queries, documents)
    ]
    return pl.pallas_call(
        kernel,
        out_shape=(
            jax.ShapeDtypeStruct((8, 3, 128), F32),
            jax.ShapeDtypeStruct((8, 3), F32),
        ),
        in_specs=[hbm, hbm, smem, smem, smem],
        out_specs=(vmem, vmem),
        scratch_shapes=[
            pltpu.VMEM((256, 128), BF16),
            pltpu.VMEM((256, 128), BF16),
            pltpu.VMEM((256, 128), BF16),
            pltpu.VMEM((256, 128), BF16),
            pltpu.VMEM((2, 8, 256, 128), BF16),
            pltpu.VMEM((16, 3, 256, 128), BF16),
            pltpu.VMEM((2, 4, 256, 128), BF16),
            pltpu.VMEM((3, 2, 1024, 128), F32),
            pltpu.VMEM((16, 8, 256), F32),
            pltpu.VMEM((16, 3, 2, 4, 256), F32),
            pltpu.VMEM((16, 8, 128), F32),
            pltpu.VMEM((2, 8, 8, 128), F32),
            pltpu.VMEM((16, 8, 128), F32),
            dma((2,)), dma((2,)), dma((3,)), dma((9,)), dma((9,)), dma((8,)), dma((8,)),
            dma((2, 4)), dma((2, 4)), dma((16,)), dma((2, 8)),
        ],
        compiler_params=pltpu.CompilerParams(
            collective_id=0, has_side_effects=True, vmem_limit_bytes=32 * 2**20
        ),
        name="late_interaction",
    )(*far, query_lens, doc_lens, positives)


def solution(mesh):
    both = ("blk", "grp")
    return jax.shard_map(
        on_device,
        mesh=mesh,
        in_specs=(P(both, None, None), P(both), P(both, None, None), P(both), P(both)),
        out_specs=(P(both, None, None), P(both, None)),
        check_vma=False,
    )
```

```python
import jax
import jax.numpy as jnp
from jax import lax
from jax.experimental import pallas as pl
from jax.experimental.pallas import tpu as pltpu
from jax.sharding import PartitionSpec as P

MESH = pl.DeviceIdType.MESH
F32 = jnp.float32
BF16 = jnp.bfloat16
EPS = 1e-06
FAR = 1e30
HEAT = 20.0
PREFIXES = (64, 96, 128)
NX, NY, NZ = 4, 8, 2
LAST = (((1,), (1,)), ((), ()))


def offset(k):
    return ((k + 1) // 2) * (2 * (k % 2) - 1)


def unit(s):
    kind = jnp.where(s < 6, jnp.where((s == 1) | (s > 3), 1, 0), jnp.where(s < 14, ((s - 6) // 2) % 2, s - 14))
    near = jnp.where(s < 2, 0, 1 + s % 2)
    k = jnp.where(s < 6, near, jnp.where(s < 14, 3 + 2 * ((s - 6) // 4) + s % 2, 7))
    return kind, k


def kernel(
    q_ref, d_ref, qlen_in, dlen_ref, pos_in, grad_ref, loss_ref,
    qlen_ref, pos_ref, q_own, d_own, q_mine, d_mine, qs, ws, ds, rd, rq, peaks, piece, parts, frame, in_sem,
    z_send, z_recv, q_send, q_recv, sib_send, sib_recv, d_send, d_recv, r_send, r_recv,
):
    blk, grp = lax.axis_index("blk"), lax.axis_index("grp")
    zl, x, y = blk // (NX * NY), (blk // NY) % NX, blk % NY
    slab, core = grp // 2, grp % 2
    slabs = lax.axis_size("grp") // 2
    direct = zl == core
    kind = jnp.where(direct, 0, 1)
    half = 1 - kind
    older = jnp.logical_and(zl == 0, core == 1)
    fetch = jnp.logical_and(older, slab > 0)
    keeps = jnp.logical_not(fetch)
    hands_on = jnp.logical_and(core == 1, slab < slabs - 1)
    to_partner = jnp.logical_not(jnp.logical_and(zl == 1, core == 1))
    from_partner = jnp.logical_not(older)
    first = jnp.maximum(zl, core)

    def at(z_, x_, y_, slab_, core_):
        return ((z_ * NX + x_) * NY + y_, slab_ * 2 + core_)

    def along_y(by):
        return at(zl, x, (y + by + NY) % NY, slab, core)

    def along_x(by):
        return at(zl, (x + by + NX) % NX, y, slab, core)

    sibling = at(zl, x, y, slab, 1 - core)
    partner = at(1 - zl, x, y, slab, core)

    def crossed(by):
        return at(1 - zl, x, (y + by + NY) % NY, slab, 1 - core)

    ahead = at(0, x, y, slab + 1, 1)

    def remote(src, dst, send, recv, to):
        return pltpu.make_async_remote_copy(
            src_ref=src, dst_ref=dst, send_sem=send, recv_sem=recv, device_id=to, device_id_type=MESH
        )

    loads = [
        pltpu.make_async_copy(q_ref, q_own, in_sem.at[0]),
        pltpu.make_async_copy(d_ref, d_own, in_sem.at[1]),
        pltpu.make_async_copy(qlen_in, qlen_ref, in_sem.at[2]),
        pltpu.make_async_copy(pos_in, pos_ref, in_sem.at[3]),
    ]
    for load in loads:
        load.start()

    barrier = pltpu.get_barrier_semaphore()

    def greet(other):
        pl.semaphore_signal(barrier, inc=1, device_id=other, device_id_type=MESH)

    for other in (sibling, along_x(1), along_x(-1), along_x(2)):
        greet(other)
    pl.when(from_partner)(lambda: greet(partner))

    for by in (1, -1, 2, -2):
        greet(along_y(by))

    @pl.when(kind == 1)
    def _():
        for by in (0, 1, -1, 2, -2):
            greet(crossed(by))

    @pl.when(fetch)
    def _():
        greet(at(0, x, y, slab - 1, 1))
        greet(at(1, x, y, slab - 1, 1))

    expected = 8 + to_partner.astype(jnp.int32) + 5 * kind + hands_on.astype(jnp.int32)

    for load in loads:
        load.wait()

    tokens = lax.broadcasted_iota(jnp.int32, (32, 128), 0)
    for i in range(8):
        rows = q_own[pl.ds(32 * i, 32), :].astype(F32)
        q_mine[pl.ds(32 * i, 32), :] = jnp.where(tokens < qlen_ref[i], rows, 0.0).astype(BF16)
    doc = d_own[...].astype(F32)
    slots = lax.broadcasted_iota(jnp.int32, (256, 128), 0)
    d_mine[...] = jnp.where(slots < dlen_ref[0], doc, doc[0:1, :]).astype(BF16)

    @pl.when(direct)
    def _():
        qs[0, 0] = q_mine[...]

    @pl.when(keeps)
    def _():
        ds[zl, 0] = d_mine[...]

    @pl.when(jnp.logical_and(keeps, older))
    def _():
        ds[1, 0] = d_mine[...]

    pl.semaphore_wait(barrier, expected)

    def partner_copy():
        return remote(d_mine, ds.at[zl, 0], z_send.at[0], z_recv.at[0], partner)

    def ahead_copy():
        return remote(d_mine, ds.at[zl, 0], z_send.at[1], z_recv.at[1 + zl], ahead)

    def behind_copy(slot):
        return remote(d_mine, ds.at[slot, 0], z_send.at[1], z_recv.at[1 + slot], ahead)

    def query_copy(k):
        return remote(q_mine, qs.at[0, k], q_send.at[k], q_recv.at[k], along_y(offset(k)))

    def cross_copy(k):
        return remote(q_mine, qs.at[1, k], q_send.at[k], q_recv.at[k], crossed(offset(k)))

    def ring_copy(k):
        low, high = pl.ds(0, 128), pl.ds(128, 128)
        if k == 7:
            src, dst, by = qs.at[kind, 3, low], qs.at[kind, 7, low], 2
        elif k == 8:
            src, dst, by = qs.at[kind, 4, high], qs.at[kind, 7, high], -2
        else:
            src, dst, by = qs.at[kind, k - 2], qs.at[kind, k], 1 if k == 5 else -1
        return remote(src, dst, q_send.at[k], q_recv.at[k], along_y(by))

    def sib_copy(k):
        return remote(qs.at[kind, k], qs.at[kind, k], sib_send.at[k], sib_recv.at[k], sibling)

    def sib_wait(k):
        remote(qs.at[1 - kind, k], qs.at[1 - kind, k], sib_send.at[k], sib_recv.at[k], sibling).wait_recv()

    def doc_copy(slot, b):
        return remote(ds.at[slot, 0], ds.at[slot, b], d_send.at[slot, b], d_recv.at[slot, b], along_x(b))

    def arrived(*ks):
        for k in ks:
            (ring_copy if k > 4 else query_copy)(k).wait_recv()
        if 3 in ks:
            for k in (5, 6, 7, 8):
                ring_copy(k).start()
        for k in ks:
            if k < 8:
                sib_copy(k).start()

    def shared(*ks):
        for k in ks:
            sib_wait(k)

    def spread(slot):
        for b in (1, 3, 2):
            doc_copy(slot, b).start()

    pl.when(to_partner)(lambda: partner_copy().start())
    pl.when(hands_on)(lambda: ahead_copy().start())

    @pl.when(direct)
    def _():
        for k in (1, 2):
            query_copy(k).start()

    @pl.when(kind == 1)
    def _():
        for k in range(3):
            cross_copy(k).start()

    @pl.when(keeps)
    def _():
        spread(first)

    @pl.when(jnp.logical_and(keeps, older))
    def _():
        spread(1 - first)

    @pl.when(direct)
    def _():
        sib_copy(0).start()
        for k in (3, 4):
            query_copy(k).start()

    @pl.when(kind == 1)
    def _():
        for k in (3, 4):
            cross_copy(k).start()

    @pl.when(fetch)
    def _():
        behind_copy(1).wait_recv()
        spread(1)
        behind_copy(0).wait_recv()
        spread(0)

    @pl.when(from_partner)
    def _():
        remote(d_mine, ds.at[1 - zl, 0], z_send.at[0], z_recv.at[0], partner).wait_recv()
        spread(1 - zl)

    lanes = lax.broadcasted_iota(jnp.int32, (256, 128), 1)
    prefix_rows = lax.broadcasted_iota(jnp.int32, (8, 128), 0)
    prefix_lanes = lax.broadcasted_iota(jnp.int32, (8, 128), 1)
    limit = jnp.where(prefix_rows == 0, 64, jnp.where(prefix_rows == 1, 96, 128))
    below = (prefix_lanes < limit).astype(F32).astype(BF16)
    seg_rows = lax.broadcasted_iota(jnp.int32, (128, 256), 0)
    seg_query = lax.broadcasted_iota(jnp.int32, (128, 256), 1) // 32

    def split(value):
        high = value.astype(BF16)
        return high, value - high.astype(F32)

    def prepare(s):
        kind_, k = unit(s)
        q = qs[kind_, k].astype(F32)
        for p in range(2):
            ws[s, p] = jnp.where(lanes < PREFIXES[p], q, 0.0).astype(BF16)
        ws[s, 2] = qs[kind_, k]
        high, rest = split(q * q)
        sums = lax.dot_general(below, high, LAST, preferred_element_type=F32)
        sums += lax.dot_general(below, rest.astype(BF16), LAST, preferred_element_type=F32)
        rq[s] = lax.rsqrt(sums + EPS) * HEAT

    wide_rows = lax.broadcasted_iota(jnp.int32, (256, 128), 0)
    ones = (lanes < jnp.where(wide_rows < 128, 64, 96)).astype(F32).astype(BF16)

    def norms(slot):
        values = ds[slot].reshape(1024, 128).astype(F32)
        squares = values * values
        high, rest = split(squares)
        sums = lax.dot_general(high, ones, LAST, preferred_element_type=F32)
        sums += lax.dot_general(rest.astype(BF16), ones, LAST, preferred_element_type=F32)
        for p in range(2):
            rd[p, slot] = lax.rsqrt(sums[:, 128 * p : 128 * p + 128] + EPS)
        total = jnp.sum(squares, axis=1, keepdims=True)
        rd[2, slot] = jnp.broadcast_to(lax.rsqrt(total + EPS), (1024, 128))

    def job(s, slot):
        docs = ds[slot].reshape(1024, 128)
        for p in range(3):
            dots = lax.dot_general(docs, ws[s, p], LAST, preferred_element_type=F32)
            scale = rd[p, slot]
            for c in range(2):
                scaled = dots[:, c * 128 : (c + 1) * 128] * scale
                best = jnp.max(jnp.max(scaled.reshape(4, 32, 8, 128), axis=1), axis=1)
                peaks[s, p, slot, :, pl.ds(c * 128, 128)] = best

    def whole_job(s):
        docs = ds[...].reshape(2048, 128)
        for p in range(3):
            dots = lax.dot_general(docs, ws[s, p], LAST, preferred_element_type=F32)
            scale = rd[p].reshape(2048, 128)
            for c in range(2):
                scaled = dots[:, c * 128 : (c + 1) * 128] * scale
                best = jnp.max(jnp.max(scaled.reshape(2, 4, 32, 8, 128), axis=2), axis=2)
                peaks[s, p, :, :, pl.ds(c * 128, 128)] = best

    def finish(s):
        total = jnp.zeros((16, 128), F32)
        for p in range(3):
            best = jnp.concatenate(
                [peaks[s + j, p].reshape(8, 256) * rq[s + j, p : p + 1, :] for j in range(2)], axis=0
            )
            seg = (seg_rows == seg_query + 8 * p).astype(F32).astype(BF16)
            high, rest = split(best)
            middle, rest = split(rest)
            parts_ = jnp.concatenate([high, middle, rest.astype(BF16)], axis=0)
            sums = lax.dot_general(parts_, seg, LAST, preferred_element_type=F32)
            total += sums[:16] + sums[16:32] + sums[32:]
        piece[s] = total[:8]
        piece[s + 1] = total[8:]

    def back_copy(s):
        kind_, k = unit(s)
        home = at(jnp.where(kind_ == 0, zl, 1 - zl), x, (y - offset(k) + NY) % NY, slab, zl)
        return remote(piece.at[s], parts.at[half, y], r_send.at[s], r_recv.at[half, k], home)

    def is_home(s):
        return jnp.logical_and(direct, s == 0)

    def send_back(s):
        pl.when(jnp.logical_not(is_home(s)))(lambda: back_copy(s).start())

        @pl.when(is_home(s))
        def _():
            parts[half, y] = piece[s]

    @pl.when(direct)
    def _():
        arrived(1, 2)
        shared(0)

    @pl.when(kind == 1)
    def _():
        arrived(0)
        shared(0, 1, 2)
        arrived(1, 2)

    def wait_docs(slot):
        for b in range(1, NX):
            doc_copy(slot, b).wait_recv()

    for s in range(4):
        prepare(jnp.int32(s))
    wait_docs(first)
    norms(first)
    for s in range(4):
        job(s, first)
    pl.when(direct)(lambda: shared(1, 2))
    for s in range(4, 6):
        prepare(jnp.int32(s))
        job(s, first)
    wait_docs(1 - first)
    pl.when(direct)(lambda: arrived(3, 4))
    norms(1 - first)
    for s in range(2, 4):
        job(s, 1 - first)

    def later(i, carry):
        s = 6 + 2 * i
        done = jnp.where(i == 0, 2, 4 + 2 * i)

        @pl.when(kind == 1)
        def _():
            @pl.when(i == 0)
            def _():
                shared(3, 4)
                arrived(3, 4)

            @pl.when(i == 2)
            def _():
                shared(5, 6)
                arrived(5, 6)

            pl.when(i == 3)(lambda: arrived(8, 7))
            pl.when(i == 4)(lambda: shared(7))

        @pl.when(direct)
        def _():
            @pl.when(i == 1)
            def _():
                shared(3, 4)
                arrived(5, 6)

            @pl.when(i == 3)
            def _():
                shared(5, 6)
                arrived(8, 7)

            pl.when(i == 4)(lambda: shared(7))

        finish(done)
        for j in range(2):
            prepare(s + j)
            whole_job(s + j)
        send_back(done)
        send_back(done + 1)
        return carry

    lax.fori_loop(0, 5, later, 0)

    finish(14)
    send_back(jnp.int32(14))
    send_back(jnp.int32(15))
    for s in (4, 5):
        job(s, 1 - first)
    finish(4)
    for s in (4, 5):
        send_back(jnp.int32(s))
    for s in (0, 1):
        job(s, 1 - first)
    finish(0)
    for s in (0, 1):
        send_back(jnp.int32(s))

    for h in range(2):
        for k in range(NY):
            back = remote(piece.at[0], parts.at[h, (y + offset(k) + NY) % NY], r_send.at[0], r_recv.at[h, k], sibling)
            if h == 1 and k == 0:
                pl.when(kind == 1)(lambda: back.wait_recv())
            else:
                back.wait_recv()

    for h in range(2):
        for slot in range(NZ):
            for b in range(NX):
                column = h * 8 + slot * 4 + (x - b + NX) % NX
                frame[column] = parts[h, :, slot * 4 + b, :]
    logits = jnp.transpose(frame[...].reshape(128, 128))
    columns = lax.broadcasted_iota(jnp.int32, (8, 128), 1)
    rows = lax.broadcasted_iota(jnp.int32, (8, 128), 0)
    valid = jnp.logical_or(columns >= 64, grp > 0)
    target = jnp.zeros((8, 128), jnp.int32)
    for i in range(8):
        target = jnp.where(rows == i, pos_ref[i] + 64, target)
    chosen = (columns == target).astype(F32)
    for p in range(3):
        value = logits[8 * p : 8 * p + 8, :]
        held = jnp.where(valid, value, -FAR)
        highest = jnp.max(held, axis=1, keepdims=True)
        weights = jnp.where(valid, jnp.exp(held - highest), 0.0)
        total = jnp.sum(weights, axis=1, keepdims=True)
        picked = jnp.sum(jnp.where(columns == target, value, 0.0), axis=1, keepdims=True)
        grad_ref[:, p, :] = weights / total - chosen
        loss_ref[:, p : p + 1] = jnp.log(total) + highest - picked

    pl.when(kind == 1)(lambda: cross_copy(0).wait_send())
    pl.when(to_partner)(lambda: partner_copy().wait_send())
    pl.when(hands_on)(lambda: ahead_copy().wait_send())
    for k in range(1, 5):
        query_copy(k).wait_send()
    for k in range(5, 9):
        ring_copy(k).wait_send()
    for k in range(NY):
        sib_copy(k).wait_send()
    for slot in range(2):
        for b in range(1, NX):
            doc_copy(slot, b).wait_send()

    def sent(s, carry):
        pl.when(jnp.logical_not(is_home(s)))(lambda: back_copy(s).wait_send())
        return carry

    lax.fori_loop(0, 16, sent, 0)


def on_device(queries, query_lens, documents, doc_lens, positives):
    vmem = pl.BlockSpec(memory_space=pltpu.VMEM)
    hbm = pl.BlockSpec(memory_space=pltpu.HBM)
    smem = pl.BlockSpec(memory_space=pltpu.SMEM)
    dma = pltpu.SemaphoreType.DMA
    q, d, q_lens, places = [
        pltpu.with_memory_space_constraint(block, pltpu.HBM)
        for block in (queries.reshape(256, 128), documents.reshape(256, 128), query_lens, positives)
    ]
    return pl.pallas_call(
        kernel,
        out_shape=(
            jax.ShapeDtypeStruct((8, 3, 128), F32),
            jax.ShapeDtypeStruct((8, 3), F32),
        ),
        in_specs=[hbm, hbm, hbm, smem, hbm],
        out_specs=(vmem, vmem),
        scratch_shapes=[
            pltpu.SMEM((8,), jnp.int32),
            pltpu.SMEM((8,), jnp.int32),
            pltpu.VMEM((256, 128), BF16),
            pltpu.VMEM((256, 128), BF16),
            pltpu.VMEM((256, 128), BF16),
            pltpu.VMEM((256, 128), BF16),
            pltpu.VMEM((2, 8, 256, 128), BF16),
            pltpu.VMEM((16, 3, 256, 128), BF16),
            pltpu.VMEM((2, 4, 256, 128), BF16),
            pltpu.VMEM((3, 2, 1024, 128), F32),
            pltpu.VMEM((16, 8, 256), F32),
            pltpu.VMEM((16, 3, 2, 4, 256), F32),
            pltpu.VMEM((16, 8, 128), F32),
            pltpu.VMEM((2, 8, 8, 128), F32),
            pltpu.VMEM((16, 8, 128), F32),
            dma((4,)), dma((2,)), dma((3,)), dma((9,)), dma((9,)), dma((8,)), dma((8,)),
            dma((2, 4)), dma((2, 4)), dma((16,)), dma((2, 8)),
        ],
        compiler_params=pltpu.CompilerParams(
            collective_id=0, has_side_effects=True, vmem_limit_bytes=32 * 2**20
        ),
        name="late_interaction",
    )(q, d, q_lens, doc_lens, places)


def solution(mesh):
    both = ("blk", "grp")
    return jax.shard_map(
        on_device,
        mesh=mesh,
        in_specs=(P(both, None, None), P(both), P(both, None, None), P(both), P(both)),
        out_specs=(P(both, None, None), P(both, None)),
        check_vma=False,
    )
```

```python
import jax
import jax.numpy as jnp
from jax import lax
from jax.experimental import pallas as pl
from jax.experimental.pallas import tpu as pltpu
from jax.sharding import PartitionSpec as P

MESH = pl.DeviceIdType.MESH
F32 = jnp.float32
BF16 = jnp.bfloat16
EPS = 1e-06
FAR = 1e30
HEAT = 20.0
PREFIXES = (64, 96, 128)
NX, NY, NZ = 4, 8, 2
LAST = (((1,), (1,)), ((), ()))


def offset(k):
    return ((k + 1) // 2) * (2 * (k % 2) - 1)


def unit(s):
    kind = jnp.where(s < 6, jnp.where((s == 1) | (s > 3), 1, 0), jnp.where(s < 14, ((s - 6) // 2) % 2, s - 14))
    near = jnp.where(s < 2, 0, 1 + s % 2)
    k = jnp.where(s < 6, near, jnp.where(s < 14, 3 + 2 * ((s - 6) // 4) + s % 2, 7))
    return kind, k


def kernel(
    q_ref, d_ref, qlen_in, dlen_ref, pos_in, grad_ref, loss_ref,
    qlen_ref, pos_ref, q_own, d_own, q_mine, d_mine, qs, ws, ds, rd, rq, peaks, piece, parts, frame, in_sem,
    z_send, z_recv, q_send, q_recv, sib_send, sib_recv, d_send, d_recv, r_send, r_recv,
):
    blk, grp = lax.axis_index("blk"), lax.axis_index("grp")
    zl, x, y = blk // (NX * NY), (blk // NY) % NX, blk % NY
    slab, core = grp // 2, grp % 2
    slabs = lax.axis_size("grp") // 2
    direct = zl == core
    kind = jnp.where(direct, 0, 1)
    half = 1 - kind
    older = jnp.logical_and(zl == 0, core == 1)
    fetch = jnp.logical_and(older, slab > 0)
    keeps = jnp.logical_not(fetch)
    hands_on = jnp.logical_and(core == 1, slab < slabs - 1)
    to_partner = jnp.logical_not(jnp.logical_and(zl == 1, core == 1))
    from_partner = jnp.logical_not(older)
    first = jnp.maximum(zl, core)

    def at(z_, x_, y_, slab_, core_):
        return ((z_ * NX + x_) * NY + y_, slab_ * 2 + core_)

    def along_y(by):
        return at(zl, x, (y + by + NY) % NY, slab, core)

    def along_x(by):
        return at(zl, (x + by + NX) % NX, y, slab, core)

    sibling = at(zl, x, y, slab, 1 - core)
    partner = at(1 - zl, x, y, slab, core)

    def crossed(by):
        return at(1 - zl, x, (y + by + NY) % NY, slab, 1 - core)

    ahead = at(0, x, y, slab + 1, 1)

    def remote(src, dst, send, recv, to):
        return pltpu.make_async_remote_copy(
            src_ref=src, dst_ref=dst, send_sem=send, recv_sem=recv, device_id=to, device_id_type=MESH
        )

    loads = [
        pltpu.make_async_copy(q_ref, q_own, in_sem.at[0]),
        pltpu.make_async_copy(d_ref, d_own, in_sem.at[1]),
        pltpu.make_async_copy(qlen_in, qlen_ref, in_sem.at[2]),
        pltpu.make_async_copy(pos_in, pos_ref, in_sem.at[3]),
    ]
    for load in loads:
        load.start()

    barrier = pltpu.get_barrier_semaphore()

    def greet(other):
        pl.semaphore_signal(barrier, inc=1, device_id=other, device_id_type=MESH)

    for other in (sibling, along_x(1), along_x(-1), along_x(2)):
        greet(other)
    pl.when(from_partner)(lambda: greet(partner))

    for by in (1, -1, 2, -2):
        greet(along_y(by))

    @pl.when(kind == 1)
    def _():
        for by in (0, 1, -1, 2, -2):
            greet(crossed(by))

    @pl.when(fetch)
    def _():
        greet(at(0, x, y, slab - 1, 1))
        greet(at(1, x, y, slab - 1, 1))

    expected = 8 + to_partner.astype(jnp.int32) + 5 * kind + hands_on.astype(jnp.int32)

    for load in loads:
        load.wait()

    doc = d_own[...].astype(F32)
    slots = lax.broadcasted_iota(jnp.int32, (256, 128), 0)
    d_mine[...] = jnp.where(slots < dlen_ref[0], doc, doc[0:1, :]).astype(BF16)

    @pl.when(keeps)
    def _():
        ds[zl, 0] = d_mine[...]

    @pl.when(jnp.logical_and(keeps, older))
    def _():
        ds[1, 0] = d_mine[...]

    pl.semaphore_wait(barrier, expected)

    def partner_copy():
        return remote(d_mine, ds.at[zl, 0], z_send.at[0], z_recv.at[0], partner)

    def ahead_copy():
        return remote(d_mine, ds.at[zl, 0], z_send.at[1], z_recv.at[1 + zl], ahead)

    def behind_copy(slot):
        return remote(d_mine, ds.at[slot, 0], z_send.at[1], z_recv.at[1 + slot], ahead)

    def query_copy(k):
        return remote(q_mine, qs.at[0, k], q_send.at[k], q_recv.at[k], along_y(offset(k)))

    def cross_copy(k):
        return remote(q_mine, qs.at[1, k], q_send.at[k], q_recv.at[k], crossed(offset(k)))

    def ring_copy(k):
        low, high = pl.ds(0, 128), pl.ds(128, 128)
        if k == 7:
            src, dst, by = qs.at[kind, 3, low], qs.at[kind, 7, low], 2
        elif k == 8:
            src, dst, by = qs.at[kind, 4, high], qs.at[kind, 7, high], -2
        else:
            src, dst, by = qs.at[kind, k - 2], qs.at[kind, k], 1 if k == 5 else -1
        return remote(src, dst, q_send.at[k], q_recv.at[k], along_y(by))

    def sib_copy(k):
        return remote(qs.at[kind, k], qs.at[kind, k], sib_send.at[k], sib_recv.at[k], sibling)

    def sib_wait(k):
        remote(qs.at[1 - kind, k], qs.at[1 - kind, k], sib_send.at[k], sib_recv.at[k], sibling).wait_recv()

    def doc_copy(slot, b):
        return remote(ds.at[slot, 0], ds.at[slot, b], d_send.at[slot, b], d_recv.at[slot, b], along_x(b))

    def arrived(*ks):
        for k in ks:
            (ring_copy if k > 4 else query_copy)(k).wait_recv()
        if 3 in ks:
            for k in (5, 6, 7, 8):
                ring_copy(k).start()
        for k in ks:
            if k < 8:
                sib_copy(k).start()

    def shared(*ks):
        for k in ks:
            sib_wait(k)

    def spread(slot):
        for b in (1, 3, 2):
            doc_copy(slot, b).start()

    pl.when(to_partner)(lambda: partner_copy().start())
    pl.when(hands_on)(lambda: ahead_copy().start())

    @pl.when(keeps)
    def _():
        spread(first)

    @pl.when(jnp.logical_and(keeps, older))
    def _():
        spread(1 - first)

    tokens = lax.broadcasted_iota(jnp.int32, (32, 128), 0)
    for i in range(8):
        rows = q_own[pl.ds(32 * i, 32), :].astype(F32)
        q_mine[pl.ds(32 * i, 32), :] = jnp.where(tokens < qlen_ref[i], rows, 0.0).astype(BF16)

    @pl.when(direct)
    def _():
        qs[0, 0] = q_mine[...]

    @pl.when(direct)
    def _():
        for k in (1, 2):
            query_copy(k).start()

    @pl.when(kind == 1)
    def _():
        for k in range(3):
            cross_copy(k).start()

    @pl.when(direct)
    def _():
        sib_copy(0).start()
        for k in (3, 4):
            query_copy(k).start()

    @pl.when(kind == 1)
    def _():
        for k in (3, 4):
            cross_copy(k).start()

    @pl.when(fetch)
    def _():
        behind_copy(1).wait_recv()
        spread(1)
        behind_copy(0).wait_recv()
        spread(0)

    @pl.when(from_partner)
    def _():
        remote(d_mine, ds.at[1 - zl, 0], z_send.at[0], z_recv.at[0], partner).wait_recv()
        spread(1 - zl)

    lanes = lax.broadcasted_iota(jnp.int32, (256, 128), 1)
    prefix_rows = lax.broadcasted_iota(jnp.int32, (8, 128), 0)
    prefix_lanes = lax.broadcasted_iota(jnp.int32, (8, 128), 1)
    limit = jnp.where(prefix_rows == 0, 64, jnp.where(prefix_rows == 1, 96, 128))
    below = (prefix_lanes < limit).astype(F32).astype(BF16)
    seg_rows = lax.broadcasted_iota(jnp.int32, (128, 256), 0)
    seg_query = lax.broadcasted_iota(jnp.int32, (128, 256), 1) // 32

    def split(value):
        high = value.astype(BF16)
        return high, value - high.astype(F32)

    def prepare(s):
        kind_, k = unit(s)
        q = qs[kind_, k].astype(F32)
        for p in range(2):
            ws[s, p] = jnp.where(lanes < PREFIXES[p], q, 0.0).astype(BF16)
        ws[s, 2] = qs[kind_, k]
        high, rest = split(q * q)
        sums = lax.dot_general(below, high, LAST, preferred_element_type=F32)
        sums += lax.dot_general(below, rest.astype(BF16), LAST, preferred_element_type=F32)
        rq[s] = lax.rsqrt(sums + EPS) * HEAT

    wide_rows = lax.broadcasted_iota(jnp.int32, (256, 128), 0)
    ones = (lanes < jnp.where(wide_rows < 128, 64, 96)).astype(F32).astype(BF16)

    def norms(slot):
        values = ds[slot].reshape(1024, 128).astype(F32)
        squares = values * values
        high, rest = split(squares)
        sums = lax.dot_general(high, ones, LAST, preferred_element_type=F32)
        sums += lax.dot_general(rest.astype(BF16), ones, LAST, preferred_element_type=F32)
        for p in range(2):
            rd[p, slot] = lax.rsqrt(sums[:, 128 * p : 128 * p + 128] + EPS)
        total = jnp.sum(squares, axis=1, keepdims=True)
        rd[2, slot] = jnp.broadcast_to(lax.rsqrt(total + EPS), (1024, 128))

    def job(s, slot):
        docs = ds[slot].reshape(1024, 128)
        for p in range(3):
            dots = lax.dot_general(docs, ws[s, p], LAST, preferred_element_type=F32)
            scale = rd[p, slot]
            for c in range(2):
                scaled = dots[:, c * 128 : (c + 1) * 128] * scale
                best = jnp.max(jnp.max(scaled.reshape(4, 32, 8, 128), axis=1), axis=1)
                peaks[s, p, slot, :, pl.ds(c * 128, 128)] = best

    def whole_job(s):
        docs = ds[...].reshape(2048, 128)
        for p in range(3):
            dots = lax.dot_general(docs, ws[s, p], LAST, preferred_element_type=F32)
            scale = rd[p].reshape(2048, 128)
            for c in range(2):
                scaled = dots[:, c * 128 : (c + 1) * 128] * scale
                best = jnp.max(jnp.max(scaled.reshape(2, 4, 32, 8, 128), axis=2), axis=2)
                peaks[s, p, :, :, pl.ds(c * 128, 128)] = best

    def finish(s):
        total = jnp.zeros((16, 128), F32)
        for p in range(3):
            best = jnp.concatenate(
                [peaks[s + j, p].reshape(8, 256) * rq[s + j, p : p + 1, :] for j in range(2)], axis=0
            )
            seg = (seg_rows == seg_query + 8 * p).astype(F32).astype(BF16)
            high, rest = split(best)
            middle, rest = split(rest)
            parts_ = jnp.concatenate([high, middle, rest.astype(BF16)], axis=0)
            sums = lax.dot_general(parts_, seg, LAST, preferred_element_type=F32)
            total += sums[:16] + sums[16:32] + sums[32:]
        piece[s] = total[:8]
        piece[s + 1] = total[8:]

    def back_copy(s):
        kind_, k = unit(s)
        home = at(jnp.where(kind_ == 0, zl, 1 - zl), x, (y - offset(k) + NY) % NY, slab, zl)
        return remote(piece.at[s], parts.at[half, y], r_send.at[s], r_recv.at[half, k], home)

    def is_home(s):
        return jnp.logical_and(direct, s == 0)

    def send_back(s):
        pl.when(jnp.logical_not(is_home(s)))(lambda: back_copy(s).start())

        @pl.when(is_home(s))
        def _():
            parts[half, y] = piece[s]

    @pl.when(direct)
    def _():
        arrived(1, 2)
        shared(0)

    @pl.when(kind == 1)
    def _():
        arrived(0)
        shared(0, 1, 2)
        arrived(1, 2)

    def wait_docs(slot):
        for b in range(1, NX):
            doc_copy(slot, b).wait_recv()

    for s in range(4):
        prepare(jnp.int32(s))
    wait_docs(first)
    norms(first)
    for s in range(4):
        job(s, first)
    pl.when(direct)(lambda: shared(1, 2))
    for s in range(4, 6):
        prepare(jnp.int32(s))
        job(s, first)
    wait_docs(1 - first)
    pl.when(direct)(lambda: arrived(3, 4))
    norms(1 - first)
    for s in range(2, 4):
        job(s, 1 - first)

    def later(i, carry):
        s = 6 + 2 * i
        done = jnp.where(i == 0, 2, 4 + 2 * i)

        @pl.when(kind == 1)
        def _():
            @pl.when(i == 0)
            def _():
                shared(3, 4)
                arrived(3, 4)

            @pl.when(i == 2)
            def _():
                shared(5, 6)
                arrived(5, 6)

            pl.when(i == 3)(lambda: arrived(8, 7))
            pl.when(i == 4)(lambda: shared(7))

        @pl.when(direct)
        def _():
            @pl.when(i == 1)
            def _():
                shared(3, 4)
                arrived(5, 6)

            @pl.when(i == 3)
            def _():
                shared(5, 6)
                arrived(8, 7)

            pl.when(i == 4)(lambda: shared(7))

        finish(done)
        for j in range(2):
            prepare(s + j)
            whole_job(s + j)
        send_back(done)
        send_back(done + 1)
        return carry

    lax.fori_loop(0, 5, later, 0)

    finish(14)
    send_back(jnp.int32(14))
    send_back(jnp.int32(15))
    for s in (4, 5):
        job(s, 1 - first)
    finish(4)
    for s in (4, 5):
        send_back(jnp.int32(s))
    for s in (0, 1):
        job(s, 1 - first)
    finish(0)
    for s in (0, 1):
        send_back(jnp.int32(s))

    for h in range(2):
        for k in range(NY):
            back = remote(piece.at[0], parts.at[h, (y + offset(k) + NY) % NY], r_send.at[0], r_recv.at[h, k], sibling)
            if h == 1 and k == 0:
                pl.when(kind == 1)(lambda: back.wait_recv())
            else:
                back.wait_recv()

    for h in range(2):
        for slot in range(NZ):
            for b in range(NX):
                column = h * 8 + slot * 4 + (x - b + NX) % NX
                frame[column] = parts[h, :, slot * 4 + b, :]
    logits = jnp.transpose(frame[...].reshape(128, 128))
    columns = lax.broadcasted_iota(jnp.int32, (8, 128), 1)
    rows = lax.broadcasted_iota(jnp.int32, (8, 128), 0)
    valid = jnp.logical_or(columns >= 64, grp > 0)
    target = jnp.zeros((8, 128), jnp.int32)
    for i in range(8):
        target = jnp.where(rows == i, pos_ref[i] + 64, target)
    chosen = (columns == target).astype(F32)
    for p in range(3):
        value = logits[8 * p : 8 * p + 8, :]
        held = jnp.where(valid, value, -FAR)
        highest = jnp.max(held, axis=1, keepdims=True)
        weights = jnp.where(valid, jnp.exp(held - highest), 0.0)
        total = jnp.sum(weights, axis=1, keepdims=True)
        picked = jnp.sum(jnp.where(columns == target, value, 0.0), axis=1, keepdims=True)
        grad_ref[:, p, :] = weights / total - chosen
        loss_ref[:, p : p + 1] = jnp.log(total) + highest - picked

    pl.when(kind == 1)(lambda: cross_copy(0).wait_send())
    pl.when(to_partner)(lambda: partner_copy().wait_send())
    pl.when(hands_on)(lambda: ahead_copy().wait_send())
    for k in range(1, 5):
        query_copy(k).wait_send()
    for k in range(5, 9):
        ring_copy(k).wait_send()
    for k in range(NY):
        sib_copy(k).wait_send()
    for slot in range(2):
        for b in range(1, NX):
            doc_copy(slot, b).wait_send()

    def sent(s, carry):
        pl.when(jnp.logical_not(is_home(s)))(lambda: back_copy(s).wait_send())
        return carry

    lax.fori_loop(0, 16, sent, 0)


def on_device(queries, query_lens, documents, doc_lens, positives):
    vmem = pl.BlockSpec(memory_space=pltpu.VMEM)
    hbm = pl.BlockSpec(memory_space=pltpu.HBM)
    smem = pl.BlockSpec(memory_space=pltpu.SMEM)
    dma = pltpu.SemaphoreType.DMA
    q, d, q_lens, places = [
        pltpu.with_memory_space_constraint(block, pltpu.HBM)
        for block in (queries.reshape(256, 128), documents.reshape(256, 128), query_lens, positives)
    ]
    return pl.pallas_call(
        kernel,
        out_shape=(
            jax.ShapeDtypeStruct((8, 3, 128), F32),
            jax.ShapeDtypeStruct((8, 3), F32),
        ),
        in_specs=[hbm, hbm, hbm, smem, hbm],
        out_specs=(vmem, vmem),
        scratch_shapes=[
            pltpu.SMEM((8,), jnp.int32),
            pltpu.SMEM((8,), jnp.int32),
            pltpu.VMEM((256, 128), BF16),
            pltpu.VMEM((256, 128), BF16),
            pltpu.VMEM((256, 128), BF16),
            pltpu.VMEM((256, 128), BF16),
            pltpu.VMEM((2, 8, 256, 128), BF16),
            pltpu.VMEM((16, 3, 256, 128), BF16),
            pltpu.VMEM((2, 4, 256, 128), BF16),
            pltpu.VMEM((3, 2, 1024, 128), F32),
            pltpu.VMEM((16, 8, 256), F32),
            pltpu.VMEM((16, 3, 2, 4, 256), F32),
            pltpu.VMEM((16, 8, 128), F32),
            pltpu.VMEM((2, 8, 8, 128), F32),
            pltpu.VMEM((16, 8, 128), F32),
            dma((4,)), dma((2,)), dma((3,)), dma((9,)), dma((9,)), dma((8,)), dma((8,)),
            dma((2, 4)), dma((2, 4)), dma((16,)), dma((2, 8)),
        ],
        compiler_params=pltpu.CompilerParams(
            collective_id=0, has_side_effects=True, vmem_limit_bytes=32 * 2**20
        ),
        name="late_interaction",
    )(q, d, q_lens, doc_lens, places)


def solution(mesh):
    both = ("blk", "grp")
    return jax.shard_map(
        on_device,
        mesh=mesh,
        in_specs=(P(both, None, None), P(both), P(both, None, None), P(both), P(both)),
        out_specs=(P(both, None, None), P(both, None)),
        check_vma=False,
    )
```
